256 devices in a mesh: pb: 32 (over z, x), kv: 2 (over core), ha: 4 (over y).
Axes of the slice: x: 4, y: 4, z: 8, core: 2. Of those that a mesh axis runs over, the one named last changes fastest.
Arguments:
- queries: bfloat16 [2, 4096, 3072], P('kv', 'pb', 'ha'), may hold values from -40 to 40
- keys: bfloat16 [2, 4096, 3072], P('kv', 'pb', 'ha'), may hold values from -40 to 40
- values: bfloat16 [2, 4096, 3072], P('kv', 'pb', 'ha'), may hold values from -6 to 6
- out_grad: bfloat16 [2, 4096, 3072], P('kv', 'pb', 'ha'), may hold values from -6 to 6
- block_order: int32 [2, 64], P('kv'), may hold values from 0 to 63, each once within a row
Outputs:
- attended: bfloat16 [2, 4096, 3072], P('kv', 'pb', 'ha')
- q_grad: bfloat16 [2, 4096, 3072], P('kv', 'pb', 'ha')
- k_grad: bfloat16 [2, 4096, 3072], P('kv', 'pb', 'ha')
- v_grad: bfloat16 [2, 4096, 3072], P('kv', 'pb', 'ha')
The draws below stay inside these ranges and needn't reach their ends.
Inputs may be any that keep to these rules, and one draw needn't show every extreme that they name: Each row of block_order holds every block number once.
All inputs are finite; a program needn't handle non-finite values.
Results may differ from the reference program's by a relative error of at most 0.02.
Values may be sent and summed in bfloat16 or wider, within the bound.
No kernel may reach another device: no remote copies, remote signals or barrier semaphores. Data moves between devices by JAX's collectives and lax.ppermute only.
A program may use at most 128 MiB of HBM per device.

```python
import math
import jax
import jax.numpy as jnp
from jax import lax

DH = 128
BLK = 64
HEADS = 24
SEQ = 4096
BATCH = 2
NB = 64


def draw_queries(key, part):
    key = jax.random.fold_in(key, 11)
    own = jax.random.normal(key, (BATCH, SEQ, HEADS * DH), jnp.float32)
    return (2.0 * own).astype(jnp.bfloat16)


def draw_keys(key, part):
    key = jax.random.fold_in(key, 12)
    own = jax.random.normal(key, (BATCH, SEQ, HEADS * DH), jnp.float32)
    return own.astype(jnp.bfloat16)


def steps_of(stream_key, extent, cuts, smallest, top_value):
    loudness = 1.0
    for position, blocks in cuts:
        draws = jax.random.uniform(jax.random.fold_in(jax.random.fold_in(stream_key, 6), position), (blocks,), jnp.float32, smallest / len(cuts), top_value / len(cuts))
        loudness = loudness * jnp.repeat(jnp.exp(draws), extent[position] // blocks).reshape((-1,) + (1,) * (len(extent) - 1 - position))
    return loudness


def gaussian(stream_key, extent, deviation, most, split=(), held_as=jnp.bfloat16):
    level = steps_of(stream_key, extent, split, -0.22, 0.18) if split else 1.0
    values = jax.random.normal(stream_key, extent, jnp.float32) * deviation * level
    return jnp.minimum(jnp.maximum(values, -most), most).astype(held_as)


def setup_inputs(seed: int = 0) -> dict:
    key_of = jax.random.split(jax.random.key(seed), 6)
    return {
        "queries": draw_queries(jax.random.fold_in(key_of[5], 71), 0),
        "keys": draw_keys(jax.random.fold_in(key_of[5], 71), 0),
        "values": gaussian(key_of[2], (BATCH, SEQ, HEADS * DH), 1.0, 6.0, ((0, 2), (1, 32), (2, 4))),
        "out_grad": gaussian(key_of[3], (BATCH, SEQ, HEADS * DH), 1.0, 6.0, ((0, 2), (1, 32), (2, 4))),
        "block_order": jax.vmap(lambda own: jax.random.permutation(own, NB))(jax.random.split(key_of[4], BATCH)).reshape((BATCH, NB)).astype(jnp.int32),
    }


def make_positions(order_row):
    starts = jnp.repeat(order_row * BLK, BLK)
    within = jnp.tile(jnp.arange(BLK, dtype=jnp.int32), NB)
    return (starts + within).astype(jnp.int32)

def one_head(query_rows, key_rows, value_rows, grad_rows, allowed):
    score_scale = 1.0 / math.sqrt(DH)
    scores = jnp.dot(query_rows, key_rows.T, preferred_element_type=jnp.float32) * score_scale
    scores = jnp.where(allowed, scores, jnp.float32(-1e+30))
    row_max = lax.optimization_barrier(jnp.max(scores, axis=1))
    expo = jnp.exp(scores - row_max[:, None])
    totals = lax.optimization_barrier(jnp.sum(expo, axis=1))
    numer = jnp.dot(expo.astype(jnp.bfloat16), value_rows, preferred_element_type=jnp.float32)
    attended = (numer / totals[:, None]).astype(jnp.bfloat16)
    probs = expo / totals[:, None]
    dsum = lax.optimization_barrier(jnp.sum(grad_rows.astype(jnp.float32) * attended.astype(jnp.float32), axis=1))
    dprob = jnp.dot(grad_rows, value_rows.T, preferred_element_type=jnp.float32)
    dscore = (probs * (dprob - dsum[:, None])).astype(jnp.bfloat16)
    probs_low = probs.astype(jnp.bfloat16)
    q_grad = (jnp.dot(dscore, key_rows, preferred_element_type=jnp.float32) * score_scale).astype(jnp.bfloat16)
    k_grad = (jnp.dot(dscore.T, query_rows, preferred_element_type=jnp.float32) * score_scale).astype(jnp.bfloat16)
    v_grad = jnp.dot(probs_low.T, grad_rows, preferred_element_type=jnp.float32).astype(jnp.bfloat16)
    return (attended, q_grad, k_grad, v_grad)

def split_heads(array):
    return array.reshape(SEQ, HEADS, DH).transpose(1, 0, 2)

def merge_heads(array):
    return array.transpose(1, 0, 2).reshape(SEQ, HEADS * DH)

def one_trajectory(items):
    query_all, key_all, value_all, grad_all, order_row = items
    pos = make_positions(order_row)
    allowed = pos[None, :] <= pos[:, None]

    def per_head(parts):
        return one_head(parts[0], parts[1], parts[2], parts[3], allowed)
    results = lax.map(per_head, (split_heads(query_all), split_heads(key_all), split_heads(value_all), split_heads(grad_all)))
    return (merge_heads(results[0]), merge_heads(results[1]), merge_heads(results[2]), merge_heads(results[3]))

def reference(queries, keys, values, out_grad, block_order):
    results = lax.map(one_trajectory, (queries, keys, values, out_grad, block_order))
    return (results[0], results[1], results[2], results[3])
```

```python
import math

import jax
import jax.numpy as jnp
import numpy as np
from jax import lax
from jax.experimental import pallas as pl
from jax.experimental.pallas import tpu as pltpu
from jax.sharding import Mesh
from jax.sharding import PartitionSpec as P

DH = 128
BLK = 64
SCALE = 1.0 / math.sqrt(DH)
SCALE2 = SCALE * math.log2(math.e)
GROUP = 4
ROWS = GROUP * BLK
WIDE = 512
F32 = jnp.float32
BF16 = jnp.bfloat16


def mm(a, b):
    return jnp.dot(a, b, preferred_element_type=F32)


def mm_nt(a, b):
    return lax.dot_general(a, b, (((1,), (1,)), ((), ())), preferred_element_type=F32)


def mm_tn(a, b):
    return lax.dot_general(a, b, (((0,), (0,)), ((), ())), preferred_element_type=F32)


def attention_kernel(
    nz, nx, order, me, qg, kv0, kv1, kv3, kv2a, kv2b,
    oq, o0, o1, o2, o3,
    ks, vs, qs, gs, scr, dka, dva, qacc, oacc, rowpos, sblk, spos,
):
    x = me[0]
    per_part = 2 * nz
    half = per_part // 2
    seq = ks.shape[0]

    def block_of(part, j):
        src = lax.rem(x - part + nx, nx)
        return order[((j // 2) * nx + src) * 2 + j % 2]

    def part_rows(part, j):
        if part == 2:
            ref, i = (kv2a, j) if j < half else (kv2b, j - half)
        else:
            ref, i = (kv0, kv1, None, kv3)[part], j
        return ref, i * BLK

    for part in range(nx):
        for j in range(per_part):
            p = block_of(part, j)
            ref, start = part_rows(part, j)
            at = pl.ds(pl.multiple_of(p * BLK, BLK), BLK)
            ks[at, :] = ref[start:start + BLK, :DH]
            vs[at, :] = ref[start:start + BLK, DH:]

    own = [block_of(0, j) for j in range(per_part)]
    for j in range(per_part):
        rank = jnp.int32(0)
        for i in range(per_part):
            if i != j:
                rank = rank + (own[i] < own[j]).astype(jnp.int32)
        sblk[rank] = jnp.int32(j)
        spos[rank] = own[j]
        at = pl.ds(pl.multiple_of(rank * BLK, BLK), BLK)
        qs[at, :] = qg[j * BLK:(j + 1) * BLK, :DH]
        gs[at, :] = qg[j * BLK:(j + 1) * BLK, DH:]

    dka[...] = jnp.zeros_like(dka)
    dva[...] = jnp.zeros_like(dva)

    def group_step(g, carry):
        base = g * GROUP
        lowest = spos[base]
        highest = spos[base + GROUP - 1]
        full = (lowest * BLK) // WIDE
        count = ((highest + 1) * BLK + WIDE - 1) // WIDE
        for k in range(GROUP):
            within = lax.broadcasted_iota(jnp.int32, (BLK, DH), 0)
            rowpos[k * BLK:(k + 1) * BLK, :] = within + spos[base + k] * BLK
        at = pl.ds(pl.multiple_of(base * BLK, ROWS), ROWS)
        q = qs[at, :]
        gr = gs[at, :]

        def chunk(c):
            return pl.ds(pl.multiple_of(c * WIDE, WIDE), WIDE)

        def fold(op, s):
            r = s[:, :DH]
            for i in range(1, WIDE // DH):
                r = op(r, s[:, i * DH:(i + 1) * DH])
            return r

        def score_step(masked):
            def step(c, m):
                s = mm_nt(q, ks[chunk(c), :])
                if masked:
                    pos = rowpos[:, :1]
                    key = lax.broadcasted_iota(jnp.int32, (ROWS, WIDE), 1) + c * WIDE
                    s = jnp.where(key <= pos, s, F32(-1e30))
                scr[:, chunk(c)] = s
                return jnp.maximum(m, fold(jnp.maximum, s))
            return step

        m = jnp.full((ROWS, DH), -1e30, F32)
        m = lax.fori_loop(0, full, score_step(False), m)
        m = lax.fori_loop(full, count, score_step(True), m)
        top = jnp.max(m, axis=1, keepdims=True)

        oacc[...] = jnp.zeros_like(oacc)

        def expo_step(c, tot):
            e = jnp.exp2((scr[:, chunk(c)] - top) * F32(SCALE2))
            scr[:, chunk(c)] = e
            oacc[...] += mm(e.astype(BF16), vs[chunk(c), :])
            return tot + fold(jnp.add, e)

        tot = lax.fori_loop(0, count, expo_step, jnp.zeros((ROWS, DH), F32))
        total = jnp.sum(tot, axis=1, keepdims=True)
        inv = 1.0 / total
        att = (oacc[...] / total).astype(BF16)
        dsum = jnp.sum(gr.astype(F32) * att.astype(F32), axis=1, keepdims=True)
        qacc[...] = jnp.zeros_like(qacc)

        def back_step(c, carry):
            dp = mm_nt(gr, vs[chunk(c), :])
            p = scr[:, chunk(c)] * inv
            ds = (p * (dp - dsum)).astype(BF16)
            pb = p.astype(BF16)
            qacc[...] += mm(ds, ks[chunk(c), :])
            dka[chunk(c), :] += mm_tn(ds, q)
            dva[chunk(c), :] += mm_tn(pb, gr)
            return carry

        lax.fori_loop(0, count, back_step, 0)
        dq = (qacc[...] * F32(SCALE)).astype(BF16)
        for k in range(GROUP):
            to = pl.ds(pl.multiple_of(sblk[base + k] * BLK, BLK), BLK)
            oq[to, :DH] = att[k * BLK:(k + 1) * BLK, :]
            oq[to, DH:] = dq[k * BLK:(k + 1) * BLK, :]
        return carry

    lax.fori_loop(0, per_part // GROUP, group_step, 0)

    outs = (o0, o1, o2, o3)
    for part in range(nx):
        for j in range(per_part):
            p = block_of(part, j)
            at = pl.ds(pl.multiple_of(p * BLK, BLK), BLK)
            outs[part][j * BLK:(j + 1) * BLK, :DH] = (dka[at, :] * F32(SCALE)).astype(BF16)
            outs[part][j * BLK:(j + 1) * BLK, DH:] = dva[at, :].astype(BF16)


def attention(nz, nx, order, me, qg, parts):
    rows = qg.shape[0]
    seq = rows * nx
    vm = pl.BlockSpec(memory_space=pltpu.VMEM)
    sm = pl.BlockSpec(memory_space=pltpu.SMEM)
    out = jax.ShapeDtypeStruct((rows, 2 * DH), BF16)
    return pl.pallas_call(
        lambda *refs: attention_kernel(nz, nx, *refs),
        out_shape=(out,) * 5,
        in_specs=[sm, sm] + [vm] * 6,
        out_specs=(vm,) * 5,
        scratch_shapes=[
            pltpu.VMEM((seq, DH), BF16),
            pltpu.VMEM((seq, DH), BF16),
            pltpu.VMEM((rows, DH), BF16),
            pltpu.VMEM((rows, DH), BF16),
            pltpu.VMEM((ROWS, seq), F32),
            pltpu.VMEM((seq, DH), F32),
            pltpu.VMEM((seq, DH), F32),
            pltpu.VMEM((ROWS, DH), F32),
            pltpu.VMEM((ROWS, DH), F32),
            pltpu.VMEM((ROWS, DH), jnp.int32),
            pltpu.SMEM((rows // BLK,), jnp.int32),
            pltpu.SMEM((rows // BLK,), jnp.int32),
        ],
        compiler_params=pltpu.CompilerParams(vmem_limit_bytes=48 * 2**20),
        name="attention",
    )(order, me, qg, *parts)


def by_head(a, b, slots):
    rows, width = a.shape
    heads = width // DH
    both = jnp.concatenate(
        [a.reshape(rows, heads, 1, DH), b.reshape(rows, heads, 1, DH)], axis=2
    ).reshape(rows, heads, 2 * DH)
    both = both.transpose(1, 0, 2)
    return jnp.pad(both, ((0, slots - heads), (0, 0), (0, 0)))


def from_heads(stacked, heads):
    rows = stacked.shape[1]
    a = stacked[:heads, :, :DH].transpose(1, 0, 2).reshape(rows, heads * DH)
    b = stacked[:heads, :, DH:].transpose(1, 0, 2).reshape(rows, heads * DH)
    return a, b


def make_shards(nz, nx):
    def to(step):
        return [(i, (i + step) % nx) for i in range(nx)]

    def exchange(v):
        return lax.all_to_all(v, "z", 0, 0, tiled=True)

    def shards(queries, keys, values, out_grad, block_order):
        rows, width = queries.shape[1:]
        heads = width // DH
        kv = exchange(by_head(keys[0], values[0], nz)).reshape(nz * rows, 2 * DH)
        right = lax.ppermute(kv, "x", to(1))
        left = lax.ppermute(kv, "x", to(-1))
        qg = exchange(by_head(queries[0], out_grad[0], nz)).reshape(nz * rows, 2 * DH)
        cut = nz * rows // 2
        far_a = lax.ppermute(right[:cut], "x", to(1))
        far_b = lax.ppermute(left[cut:], "x", to(-1))
        me = lax.axis_index("x").astype(jnp.int32).reshape(1)
        oq, o0, o1, o2, o3 = attention(
            nz, nx, block_order[0], me, qg, (kv, right, left, far_a, far_b)
        )
        a1 = lax.ppermute(o1, "x", to(-1))
        a3 = lax.ppermute(o3, "x", to(1))
        a2 = lax.ppermute(o2, "x", to(2))
        att, q_grad = from_heads(exchange(oq.reshape(nz, rows, 2 * DH)), heads)
        total = (
            o0.astype(F32) + a1.astype(F32) + a2.astype(F32) + a3.astype(F32)
        ).astype(BF16)
        k_grad, v_grad = from_heads(exchange(total.reshape(nz, rows, 2 * DH)), heads)
        return att[None], q_grad[None], k_grad[None], v_grad[None]

    return shards


def solution(mesh):
    sizes = dict(mesh.shape)
    nx = 4
    nz = sizes["pb"] // nx
    fine = Mesh(
        np.asarray(mesh.devices).reshape(nz, nx, sizes["kv"], sizes["ha"]), ("z", "x", "kv", "ha")
    )
    split = P("kv", ("z", "x"), "ha")
    return jax.shard_map(
        make_shards(nz, nx),
        mesh=fine,
        in_specs=(split, split, split, split, P("kv", None)),
        out_specs=(split,) * 4,
        check_vma=False,
    )
```

```python
import math

import jax
import jax.numpy as jnp
import numpy as np
from jax import lax
from jax.experimental import pallas as pl
from jax.experimental.pallas import tpu as pltpu
from jax.sharding import Mesh
from jax.sharding import PartitionSpec as P

DH = 128
BLK = 64
SCALE = 1.0 / math.sqrt(DH)
SCALE2 = SCALE * math.log2(math.e)
GROUP = 8
ROWS = GROUP * BLK
WIDE = 2048
F32 = jnp.float32
BF16 = jnp.bfloat16


def mm(a, b):
    return jnp.dot(a, b, preferred_element_type=F32)


def mm_nt(a, b):
    return lax.dot_general(a, b, (((1,), (1,)), ((), ())), preferred_element_type=F32)


def attention_kernel(
    nz, nx, order, me, qg, kv0, kv1, kv3, kv2a, kv2b,
    oq, o0, o1a, o1b, o2a, o2b, o3a, o3b,
    ks, vs, qs, gs, scr, dkt, dvt, qacc, oacc, rowpos, sblk, spos,
):
    x = me[0]
    per_part = 2 * nz
    half = per_part // 2

    def block_of(part, j):
        src = lax.rem(x - part + nx, nx)
        return order[((j // 2) * nx + src) * 2 + j % 2]

    def block_rows(p):
        return pl.ds(pl.multiple_of(p * BLK, BLK), BLK)

    def part_ref(full, a, b, j):
        if full is not None:
            return full, j * BLK
        return (a, j * BLK) if j < half else (b, (j - half) * BLK)

    for part in range(nx):
        for j in range(per_part):
            ref, start = part_ref((kv0, kv1, None, kv3)[part], kv2a, kv2b, j)
            at = block_rows(block_of(part, j))
            ks[at, :] = ref[start:start + BLK, :DH]
            vs[at, :] = ref[start:start + BLK, DH:]

    own = [block_of(0, j) for j in range(per_part)]
    for j in range(per_part):
        rank = jnp.int32(0)
        for i in range(per_part):
            if i != j:
                rank = rank + (own[i] < own[j]).astype(jnp.int32)
        sblk[rank] = jnp.int32(j)
        spos[rank] = own[j]
        at = block_rows(rank)
        qs[at, :] = qg[j * BLK:(j + 1) * BLK, :DH]
        gs[at, :] = qg[j * BLK:(j + 1) * BLK, DH:]

    dkt[...] = jnp.zeros_like(dkt)
    dvt[...] = jnp.zeros_like(dvt)

    def chunk(c):
        return pl.ds(pl.multiple_of(c * WIDE, WIDE), WIDE)

    def fold(op, s):
        r = s[:, :DH]
        for i in range(1, WIDE // DH):
            r = op(r, s[:, i * DH:(i + 1) * DH])
        return r

    def group_step(g, carry):
        base = g * GROUP
        count = ((spos[base + GROUP - 1] + 1) * BLK + WIDE - 1) // WIDE
        for k in range(GROUP):
            within = lax.broadcasted_iota(jnp.int32, (BLK, DH), 0)
            rowpos[k * BLK:(k + 1) * BLK, :] = within + spos[base + k] * BLK
        at = pl.ds(pl.multiple_of(base * BLK, ROWS), ROWS)
        q = qs[at, :]
        gr = gs[at, :]
        q_t = q.T
        g_t = gr.T

        def score_step(c, m):
            s = mm_nt(q, ks[chunk(c), :])
            key = lax.broadcasted_iota(jnp.int32, (ROWS, WIDE), 1) + c * WIDE
            s = jnp.where(key <= rowpos[:, :1], s, F32(-1e30))
            scr[:, chunk(c)] = s
            return jnp.maximum(m, fold(jnp.maximum, s))

        m = lax.fori_loop(0, count, score_step, jnp.full((ROWS, DH), -1e30, F32))
        top = jnp.max(m, axis=1, keepdims=True)
        oacc[...] = jnp.zeros_like(oacc)

        def expo_step(c, tot):
            e = jnp.exp2((scr[:, chunk(c)] - top) * F32(SCALE2))
            scr[:, chunk(c)] = e
            oacc[...] += mm(e.astype(BF16), vs[chunk(c), :])
            return tot + fold(jnp.add, e)

        tot = lax.fori_loop(0, count, expo_step, jnp.zeros((ROWS, DH), F32))
        total = jnp.sum(tot, axis=1, keepdims=True)
        inv = 1.0 / total
        att = (oacc[...] / total).astype(BF16)
        dsum = jnp.sum(gr.astype(F32) * att.astype(F32), axis=1, keepdims=True)
        qacc[...] = jnp.zeros_like(qacc)

        def back_step(c, carry):
            dp = mm_nt(gr, vs[chunk(c), :])
            p = scr[:, chunk(c)] * inv
            ds = (p * (dp - dsum)).astype(BF16)
            qacc[...] += mm(ds, ks[chunk(c), :])
            dkt[:, chunk(c)] += mm(q_t, ds)
            dvt[:, chunk(c)] += mm(g_t, p.astype(BF16))
            return carry

        lax.fori_loop(0, count, back_step, 0)
        dq = (qacc[...] * F32(SCALE)).astype(BF16)
        for k in range(GROUP):
            to = block_rows(sblk[base + k])
            oq[to, :DH] = att[k * BLK:(k + 1) * BLK, :]
            oq[to, DH:] = dq[k * BLK:(k + 1) * BLK, :]
        return carry

    lax.fori_loop(0, per_part // GROUP, group_step, 0)

    for t in range(ks.shape[0] // DH):
        at = slice(t * DH, (t + 1) * DH)
        ks[at, :] = (dkt[:, at] * F32(SCALE)).T.astype(BF16)
        vs[at, :] = dvt[:, at].T.astype(BF16)

    halves = ((None, None), (o1a, o1b), (o2a, o2b), (o3a, o3b))
    for part in range(nx):
        for j in range(per_part):
            ref, start = part_ref(o0 if part == 0 else None, *halves[part], j)
            at = block_rows(block_of(part, j))
            ref[start:start + BLK, :DH] = ks[at, :]
            ref[start:start + BLK, DH:] = vs[at, :]


def attention(nz, nx, order, me, qg, parts):
    rows = qg.shape[0]
    seq = rows * nx
    vm = pl.BlockSpec(memory_space=pltpu.VMEM)
    sm = pl.BlockSpec(memory_space=pltpu.SMEM)
    whole = jax.ShapeDtypeStruct((rows, 2 * DH), BF16)
    half = jax.ShapeDtypeStruct((rows // 2, 2 * DH), BF16)
    return pl.pallas_call(
        lambda *refs: attention_kernel(nz, nx, *refs),
        out_shape=(whole,) * 2 + (half,) * 6,
        in_specs=[sm, sm] + [vm] * 6,
        out_specs=(vm,) * 8,
        scratch_shapes=[
            pltpu.VMEM((seq, DH), BF16),
            pltpu.VMEM((seq, DH), BF16),
            pltpu.VMEM((rows, DH), BF16),
            pltpu.VMEM((rows, DH), BF16),
            pltpu.VMEM((ROWS, seq), F32),
            pltpu.VMEM((DH, seq), F32),
            pltpu.VMEM((DH, seq), F32),
            pltpu.VMEM((ROWS, DH), F32),
            pltpu.VMEM((ROWS, DH), F32),
            pltpu.VMEM((ROWS, DH), jnp.int32),
            pltpu.SMEM((rows // BLK,), jnp.int32),
            pltpu.SMEM((rows // BLK,), jnp.int32),
        ],
        compiler_params=pltpu.CompilerParams(vmem_limit_bytes=48 * 2**20),
        name="attention",
    )(order, me, qg, *parts)


def run_copies(copies, sems):
    started = [pltpu.make_async_copy(src, dst, sems.at[i]) for i, (src, dst) in enumerate(copies)]
    for copy in started:
        copy.start()
    for copy in started:
        copy.wait()


def by_head(a, b, slots):
    rows, width = a.shape
    heads = width // DH

    def kernel(a_ref, b_ref, out, sems):
        copies = []
        for slot in range(slots):
            cols = slice((slot % heads) * DH, (slot % heads + 1) * DH)
            copies.append((a_ref.at[:, cols], out.at[slot, :, :DH]))
            copies.append((b_ref.at[:, cols], out.at[slot, :, DH:]))
        run_copies(copies, sems)

    anywhere = pl.BlockSpec(memory_space=pl.ANY)
    return pl.pallas_call(
        kernel,
        out_shape=jax.ShapeDtypeStruct((slots, rows, 2 * DH), BF16),
        in_specs=[anywhere, anywhere],
        out_specs=anywhere,
        scratch_shapes=[pltpu.SemaphoreType.DMA((2 * slots,))],
        name="by_head",
    )(a, b)


def from_heads(stacked, heads):
    rows = stacked.shape[1]

    def kernel(stack, a_ref, b_ref, sems):
        copies = []
        for head in range(heads):
            cols = slice(head * DH, (head + 1) * DH)
            copies.append((stack.at[head, :, :DH], a_ref.at[:, cols]))
            copies.append((stack.at[head, :, DH:], b_ref.at[:, cols]))
        run_copies(copies, sems)

    anywhere = pl.BlockSpec(memory_space=pl.ANY)
    out = jax.ShapeDtypeStruct((rows, heads * DH), BF16)
    return pl.pallas_call(
        kernel,
        out_shape=(out, out),
        in_specs=[anywhere],
        out_specs=(anywhere, anywhere),
        scratch_shapes=[pltpu.SemaphoreType.DMA((2 * heads,))],
        name="from_heads",
    )(stacked)


def make_shards(nz, nx):
    def to(step):
        return [(i, (i + step) % nx) for i in range(nx)]

    def exchange(v):
        return lax.all_to_all(v, "z", 0, 0, tiled=True)

    def shards(queries, keys, values, out_grad, block_order):
        rows, width = queries.shape[1:]
        heads = width // DH
        kv = exchange(by_head(keys[0], values[0], nz)).reshape(nz * rows, 2 * DH)
        right = lax.ppermute(kv, "x", to(1))
        left = lax.ppermute(kv, "x", to(-1))
        qg = exchange(by_head(queries[0], out_grad[0], nz)).reshape(nz * rows, 2 * DH)
        cut = nz * rows // 2
        far_a = lax.ppermute(right[:cut], "x", to(1))
        far_b = lax.ppermute(left[cut:], "x", to(-1))
        me = lax.axis_index("x").astype(jnp.int32).reshape(1)
        oq, o0, o1a, o1b, o2a, o2b, o3a, o3b = attention(
            nz, nx, block_order[0], me, qg, (kv, right, left, far_a, far_b)
        )
        via_right = lax.ppermute(o2a, "x", to(1))
        via_left = lax.ppermute(o2b, "x", to(-1))
        r3b = lax.ppermute(o3b, "x", to(1))
        r1a = lax.ppermute(o1a, "x", to(-1))
        r3a = lax.ppermute(o3a + via_right, "x", to(1))
        r1b = lax.ppermute(o1b + via_left, "x", to(-1))
        att, q_grad = from_heads(exchange(oq.reshape(nz, rows, 2 * DH)), heads)
        total_a = (o0[:cut].astype(F32) + r1a.astype(F32) + r3a.astype(F32)).astype(BF16)
        total_b = (o0[cut:].astype(F32) + r1b.astype(F32) + r3b.astype(F32)).astype(BF16)
        total = jnp.concatenate([total_a, total_b], axis=0)
        k_grad, v_grad = from_heads(exchange(total.reshape(nz, rows, 2 * DH)), heads)
        return att[None], q_grad[None], k_grad[None], v_grad[None]

    return shards


def solution(mesh):
    sizes = dict(mesh.shape)
    nx = 4
    nz = sizes["pb"] // nx
    fine = Mesh(
        np.asarray(mesh.devices).reshape(nz, nx, sizes["kv"], sizes["ha"]), ("z", "x", "kv", "ha")
    )
    split = P("kv", ("z", "x"), "ha")
    return jax.shard_map(
        make_shards(nz, nx),
        mesh=fine,
        in_specs=(split, split, split, split, P("kv", None)),
        out_specs=(split,) * 4,
        check_vma=False,
    )
```

```python
import math

import jax
import jax.numpy as jnp
import numpy as np
from jax import lax
from jax.experimental import pallas as pl
from jax.experimental.pallas import tpu as pltpu
from jax.sharding import Mesh
from jax.sharding import PartitionSpec as P

DH = 128
BLK = 64
SCALE = 1.0 / math.sqrt(DH)
SCALE2 = SCALE * math.log2(math.e)
GROUP = 8
ROWS = GROUP * BLK
WIDE = 2048
F32 = jnp.float32
BF16 = jnp.bfloat16


def mm(a, b):
    return jnp.dot(a, b, preferred_element_type=F32)


def mm_nt(a, b):
    return lax.dot_general(a, b, (((1,), (1,)), ((), ())), preferred_element_type=F32)


def attention_kernel(
    nz, nx, order, me, in0, in1, in2, in3, in4, in5, in6, in7,
    oq, o0, o1a, o1b, o2a, o2b, o3a, o3b,
    ks, vs, qs, gs, scr, dkt, dvt, qacc, oacc, rowpos, sblk, spos,
    kv0, kv1a, kv1b, kv3a, kv3b, kv2a, kv2b, qg, stage, stage_q, in_sems, out_sems,
):
    arrays = (in0, in1, in2, in3, in4, in5, in6, in7)
    landed = (kv0, kv1a, kv1b, kv3a, kv3b, kv2a, kv2b, qg)
    fetch = [
        pltpu.make_async_copy(src, dst, in_sems.at[i])
        for i, (src, dst) in enumerate(zip(arrays, landed, strict=True))
    ]
    for copy in fetch:
        copy.start()
    x = me[0]
    busy = me[1]
    per_part = 2 * nz
    half = per_part // 2

    def block_of(part, j):
        src = lax.rem(x - part + nx, nx)
        return order[(me[2 + j // 2] * nx + src) * 2 + j % 2]

    def block_rows(p):
        return pl.ds(pl.multiple_of(p * BLK, BLK), BLK)

    def part_ref(full, a, b, j):
        if full is not None:
            return full, j * BLK
        return (a, j * BLK) if j < half else (b, (j - half) * BLK)

    pieces = ((None, None), (kv1a, kv1b), (kv2a, kv2b), (kv3a, kv3b))
    arrivals = {0: (0,), 1: (1, 2), 3: (3, 4), 2: (5, 6)}
    for part in (0, 1, 3, 2):
        for i in arrivals[part]:
            fetch[i].wait()
        for j in range(per_part):
            ref, start = part_ref(kv0 if part == 0 else None, *pieces[part], j)
            at = block_rows(block_of(part, j))
            ks[at, :] = ref[start:start + BLK, :DH]
            vs[at, :] = ref[start:start + BLK, DH:]

    fetch[7].wait()
    own = [block_of(0, j) for j in range(per_part)]
    for j in range(per_part):
        rank = jnp.int32(0)
        for i in range(per_part):
            if i != j:
                rank = rank + (own[i] < own[j]).astype(jnp.int32)
        sblk[rank] = jnp.int32(j)
        spos[rank] = own[j]
        at = block_rows(rank)
        qs[at, :] = qg[j * BLK:(j + 1) * BLK, :DH]
        gs[at, :] = qg[j * BLK:(j + 1) * BLK, DH:]

    dkt[...] = jnp.zeros_like(dkt)
    dvt[...] = jnp.zeros_like(dvt)

    def chunk(c):
        return pl.ds(pl.multiple_of(c * WIDE, WIDE), WIDE)

    def fold(op, s):
        r = s[:, :DH]
        for i in range(1, WIDE // DH):
            r = op(r, s[:, i * DH:(i + 1) * DH])
        return r

    def group_step(g, carry):
        base = g * GROUP
        count = ((spos[base + GROUP - 1] + 1) * BLK + WIDE - 1) // WIDE
        for k in range(GROUP):
            within = lax.broadcasted_iota(jnp.int32, (BLK, DH), 0)
            rowpos[k * BLK:(k + 1) * BLK, :] = within + spos[base + k] * BLK
        at = pl.ds(pl.multiple_of(base * BLK, ROWS), ROWS)
        q = qs[at, :]
        gr = gs[at, :]
        q_t = q.T
        g_t = gr.T

        def score_step(c, m):
            s = mm_nt(q, ks[chunk(c), :])
            key = lax.broadcasted_iota(jnp.int32, (ROWS, WIDE), 1) + c * WIDE
            s = jnp.where(key <= rowpos[:, :1], s, F32(-1e30))
            scr[:, chunk(c)] = s
            return jnp.maximum(m, fold(jnp.maximum, s))

        m = lax.fori_loop(0, count, score_step, jnp.full((ROWS, DH), -1e30, F32))
        top = jnp.max(m, axis=1, keepdims=True)
        oacc[...] = jnp.zeros_like(oacc)

        def expo_step(c, tot):
            e = jnp.exp2((scr[:, chunk(c)] - top) * F32(SCALE2))
            scr[:, chunk(c)] = e
            oacc[...] += mm(e.astype(BF16), vs[chunk(c), :])
            return tot + fold(jnp.add, e)

        tot = lax.fori_loop(0, count, expo_step, jnp.zeros((ROWS, DH), F32))
        total = jnp.sum(tot, axis=1, keepdims=True)
        inv = 1.0 / total
        att = (oacc[...] / total).astype(BF16)
        dsum = jnp.sum(gr.astype(F32) * att.astype(F32), axis=1, keepdims=True)
        qacc[...] = jnp.zeros_like(qacc)

        def back_step(c, carry):
            dp = mm_nt(gr, vs[chunk(c), :])
            p = scr[:, chunk(c)] * inv
            ds = (p * (dp - dsum)).astype(BF16)
            qacc[...] += mm(ds, ks[chunk(c), :])
            dkt[:, chunk(c)] += mm(q_t, ds)
            dvt[:, chunk(c)] += mm(g_t, p.astype(BF16))
            return carry

        lax.fori_loop(0, count, back_step, 0)
        dq = (qacc[...] * F32(SCALE)).astype(BF16)
        for k in range(GROUP):
            to = block_rows(sblk[base + k])
            stage_q[to, :DH] = att[k * BLK:(k + 1) * BLK, :]
            stage_q[to, DH:] = dq[k * BLK:(k + 1) * BLK, :]
        return carry

    lax.fori_loop(0, (per_part // GROUP) * busy, group_step, 0)

    for t in range(ks.shape[0] // DH):
        at = slice(t * DH, (t + 1) * DH)
        ks[at, :] = (dkt[:, at] * F32(SCALE)).T.astype(BF16)
        vs[at, :] = dvt[:, at].T.astype(BF16)

    sends = [pltpu.make_async_copy(stage_q, oq, out_sems.at[8])]
    sends[0].start()
    slots = (
        (o2a, 2, 0), (o2b, 2, half), (o3b, 3, half), (o1a, 1, 0), (o3a, 3, 0), (o1b, 1, half),
        (o0.at[:half * BLK], 0, 0), (o0.at[half * BLK:], 0, half),
    )
    for i, (out, part, first) in enumerate(slots):
        for j in range(half):
            at = block_rows(block_of(part, first + j))
            stage[i, j * BLK:(j + 1) * BLK, :DH] = ks[at, :]
            stage[i, j * BLK:(j + 1) * BLK, DH:] = vs[at, :]
        sends.append(pltpu.make_async_copy(stage.at[i], out, out_sems.at[i]))
        sends[-1].start()
    for copy in sends:
        copy.wait()


def attention(nz, nx, order, me, qg, kv, near, far):
    rows = qg.shape[0]
    seq = rows * nx
    sm = pl.BlockSpec(memory_space=pltpu.SMEM)
    anywhere = pl.BlockSpec(memory_space=pl.ANY)
    hbm = pl.BlockSpec(memory_space=pltpu.HBM)
    whole = pltpu.HBM((rows, 2 * DH), BF16)
    half = pltpu.HBM((rows // 2, 2 * DH), BF16)
    return pl.pallas_call(
        lambda *refs: attention_kernel(nz, nx, *refs),
        out_shape=(whole,) * 2 + (half,) * 6,
        in_specs=[sm, sm] + [anywhere] * 8,
        out_specs=(hbm,) * 8,
        scratch_shapes=[
            pltpu.VMEM((seq, DH), BF16),
            pltpu.VMEM((seq, DH), BF16),
            pltpu.VMEM((rows, DH), BF16),
            pltpu.VMEM((rows, DH), BF16),
            pltpu.VMEM((ROWS, seq), F32),
            pltpu.VMEM((DH, seq), F32),
            pltpu.VMEM((DH, seq), F32),
            pltpu.VMEM((ROWS, DH), F32),
            pltpu.VMEM((ROWS, DH), F32),
            pltpu.VMEM((ROWS, DH), jnp.int32),
            pltpu.SMEM((rows // BLK,), jnp.int32),
            pltpu.SMEM((rows // BLK,), jnp.int32),
            pltpu.VMEM((rows, 2 * DH), BF16),
        ]
        + [pltpu.VMEM((rows // 2, 2 * DH), BF16)] * 6
        + [
            pltpu.VMEM((rows, 2 * DH), BF16),
            pltpu.VMEM((8, rows // 2, 2 * DH), BF16),
            pltpu.VMEM((rows, 2 * DH), BF16),
            pltpu.SemaphoreType.DMA((8,)),
            pltpu.SemaphoreType.DMA((9,)),
        ],
        compiler_params=pltpu.CompilerParams(vmem_limit_bytes=36 * 2**20),
        name="attention",
    )(order, me, kv, *near, *far, qg)


def by_head(a, b, slots):
    rows, width = a.shape
    heads = width // DH

    def kernel(a_ref, b_ref, out):
        for slot in range(slots):
            head = (slot + 2 * heads - slots) % heads
            cols = slice(head * DH, (head + 1) * DH)
            out[slot, :, :DH] = a_ref[:, cols]
            out[slot, :, DH:] = b_ref[:, cols]

    vm = pl.BlockSpec(memory_space=pltpu.VMEM)
    return pl.pallas_call(
        kernel,
        out_shape=pltpu.VMEM((slots, rows, 2 * DH), BF16),
        in_specs=[vm, vm],
        out_specs=vm,
        name="by_head",
    )(a, b)


def from_heads(stacked, heads):
    slots, rows = stacked.shape[:2]
    first = slots - heads

    def kernel(stack, a_ref, b_ref, got, a_own, b_own, sems):
        fetch = [
            pltpu.make_async_copy(stack.at[first + head], got.at[head], sems.at[head])
            for head in range(heads)
        ]
        for copy in fetch:
            copy.start()
        for head in range(heads):
            fetch[head].wait()
            cols = slice(head * DH, (head + 1) * DH)
            a_own[:, cols] = got[head, :, :DH]
            b_own[:, cols] = got[head, :, DH:]
        sends = [
            pltpu.make_async_copy(a_own, a_ref, sems.at[heads]),
            pltpu.make_async_copy(b_own, b_ref, sems.at[heads + 1]),
        ]
        for copy in sends:
            copy.start()
        for copy in sends:
            copy.wait()

    hbm = pl.BlockSpec(memory_space=pltpu.HBM)
    out = pltpu.HBM((rows, heads * DH), BF16)
    return pl.pallas_call(
        kernel,
        out_shape=(out, out),
        in_specs=[pl.BlockSpec(memory_space=pl.ANY)],
        out_specs=(hbm, hbm),
        scratch_shapes=[
            pltpu.VMEM((heads, rows, 2 * DH), BF16),
            pltpu.VMEM((rows, heads * DH), BF16),
            pltpu.VMEM((rows, heads * DH), BF16),
            pltpu.SemaphoreType.DMA((heads + 2,)),
        ],
        name="from_heads",
    )(stacked)


def ring_orders(nz):
    first = list(range(0, nz, 2)) + list(range(nz - 1, 0, -2))
    turn = nz // 4
    return first, first[turn:] + first[:turn]


def make_shards(nz, nx):
    def to(step):
        return [(i, (i + step) % nx) for i in range(nx)]

    rings = ring_orders(nz)
    groups = [[z * len(rings) + core for z in ring] for core, ring in enumerate(rings)]

    def exchange(v):
        return lax.all_to_all(v, ("z", "kv"), 0, 0, axis_index_groups=groups, tiled=True)

    def shards(queries, keys, values, out_grad, block_order):
        rows, width = queries.shape[1:]
        heads = width // DH
        kv = exchange(by_head(keys[0], values[0], nz)).reshape(nz * rows, 2 * DH)
        cut = nz * rows // 2
        kva, kvb = kv[:cut], kv[cut:]
        right_a = lax.ppermute(kva, "x", to(1))
        left_b = lax.ppermute(kvb, "x", to(-1))
        right_b = lax.ppermute(kvb, "x", to(1))
        left_a = lax.ppermute(kva, "x", to(-1))
        far_a = lax.ppermute(right_a, "x", to(1))
        far_b = lax.ppermute(left_b, "x", to(-1))
        qg = exchange(by_head(queries[0], out_grad[0], nz)).reshape(nz * rows, 2 * DH)
        ring = jnp.asarray(rings, jnp.int32)[lax.axis_index("kv")]
        idle = jnp.any(ring[:nz - heads] == lax.axis_index("z"))
        place = jnp.stack([lax.axis_index("x").astype(jnp.int32), 1 - idle.astype(jnp.int32)])
        me = jnp.concatenate([place, ring])
        oq, o0, o1a, o1b, o2a, o2b, o3a, o3b = attention(
            nz, nx, block_order[0], me, qg, kv, (right_a, right_b, left_a, left_b), (far_a, far_b)
        )
        via_right = lax.ppermute(o2a, "x", to(1))
        via_left = lax.ppermute(o2b, "x", to(-1))
        r3b = lax.ppermute(o3b, "x", to(1))
        r1a = lax.ppermute(o1a, "x", to(-1))
        r3a = lax.ppermute(o3a + via_right, "x", to(1))
        r1b = lax.ppermute(o1b + via_left, "x", to(-1))
        att, q_grad = from_heads(exchange(oq.reshape(nz, rows, 2 * DH)), heads)
        total_a = (o0[:cut].astype(F32) + r1a.astype(F32) + r3a.astype(F32)).astype(BF16)
        total_b = (o0[cut:].astype(F32) + r1b.astype(F32) + r3b.astype(F32)).astype(BF16)
        total = jnp.concatenate([total_a, total_b], axis=0)
        k_grad, v_grad = from_heads(exchange(total.reshape(nz, rows, 2 * DH)), heads)
        return att[None], q_grad[None], k_grad[None], v_grad[None]

    return shards


def solution(mesh):
    sizes = dict(mesh.shape)
    nx = 4
    nz = sizes["pb"] // nx
    fine = Mesh(
        np.asarray(mesh.devices).reshape(nz, nx, sizes["kv"], sizes["ha"]), ("z", "x", "kv", "ha")
    )
    split = P("kv", ("z", "x"), "ha")
    return jax.shard_map(
        make_shards(nz, nx),
        mesh=fine,
        in_specs=(split, split, split, split, P("kv", None)),
        out_specs=(split,) * 4,
        check_vma=False,
    )
```

```python
import math

import jax
import jax.numpy as jnp
import numpy as np
from jax import lax
from jax.experimental import pallas as pl
from jax.experimental.pallas import tpu as pltpu
from jax.sharding import Mesh
from jax.sharding import PartitionSpec as P

DH = 128
BLK = 64
SCALE = 1.0 / math.sqrt(DH)
SCALE2 = SCALE * math.log2(math.e)
GROUP = 8
ROWS = GROUP * BLK
WIDE = 2048
NARROW = 512
F32 = jnp.float32
BF16 = jnp.bfloat16


def mm(a, b):
    return jnp.dot(a, b, preferred_element_type=F32)


def mm_nt(a, b):
    return lax.dot_general(a, b, (((1,), (1,)), ((), ())), preferred_element_type=F32)


def attention_kernel(
    nz, nx, me, in0, in1, in2, in3, in4, in5, in6, in7,
    oq, o0, o1a, o1b, o2a, o2b, o3a, o3b,
    ks, vs, qs, gs, scr, dkt, dvt, qacc, oacc, rowpos, sblk, spos,
    kv0, kv1a, kv1b, kv3a, kv3b, kv2a, kv2b, qg, stage, stage_q, in_sems, out_sems,
):
    arrays = (in0, in1, in2, in3, in4, in5, in6, in7)
    landed = (kv0, kv1a, kv1b, kv3a, kv3b, kv2a, kv2b, qg)
    fetch = [
        pltpu.make_async_copy(src, dst, in_sems.at[i])
        for i, (src, dst) in enumerate(zip(arrays, landed, strict=True))
    ]
    for copy in fetch:
        copy.start()
    x = me[0]
    busy = me[1]
    order = me.at[2 + nz:]
    per_part = 2 * nz
    half = per_part // 2

    def block_of(part, j):
        src = lax.rem(x - part + nx, nx)
        return order[(me[2 + j // 2] * nx + src) * 2 + j % 2]

    def block_rows(p):
        return pl.ds(pl.multiple_of(p * BLK, BLK), BLK)

    def part_ref(full, a, b, j):
        if full is not None:
            return full, j * BLK
        return (a, j * BLK) if j < half else (b, (j - half) * BLK)

    pieces = ((None, None), (kv1a, kv1b), (kv2a, kv2b), (kv3a, kv3b))
    arrivals = {0: (0,), 1: (1, 2), 3: (3, 4), 2: (5, 6)}
    for part in (0, 1, 3, 2):
        for i in arrivals[part]:
            fetch[i].wait()
        for j in range(per_part):
            ref, start = part_ref(kv0 if part == 0 else None, *pieces[part], j)
            at = block_rows(block_of(part, j))
            ks[at, :] = ref[start:start + BLK, :DH]
            vs[at, :] = ref[start:start + BLK, DH:]

    fetch[7].wait()
    own = [block_of(0, j) for j in range(per_part)]
    for j in range(per_part):
        rank = jnp.int32(0)
        for i in range(per_part):
            if i != j:
                rank = rank + (own[i] < own[j]).astype(jnp.int32)
        sblk[rank] = jnp.int32(j)
        spos[rank] = own[j]
        at = block_rows(rank)
        qs[at, :] = qg[j * BLK:(j + 1) * BLK, :DH]
        gs[at, :] = qg[j * BLK:(j + 1) * BLK, DH:]

    dkt[...] = jnp.zeros_like(dkt)
    dvt[...] = jnp.zeros_like(dvt)

    def fold(op, s):
        r = s[:, :DH]
        for i in range(1, s.shape[1] // DH):
            r = op(r, s[:, i * DH:(i + 1) * DH])
        return r

    def group_step(g, carry):
        base = g * GROUP
        tiles = ((spos[base + GROUP - 1] + 1) * BLK + NARROW - 1) // NARROW
        wide = tiles // (WIDE // NARROW)
        rest = tiles % (WIDE // NARROW)
        for k in range(GROUP):
            within = lax.broadcasted_iota(jnp.int32, (BLK, DH), 0)
            rowpos[k * BLK:(k + 1) * BLK, :] = within + spos[base + k] * BLK
        at = pl.ds(pl.multiple_of(base * BLK, ROWS), ROWS)
        q = qs[at, :]
        gr = gs[at, :]
        q_t = q.T
        g_t = gr.T

        def sweep(step, value):
            def over(width, offset):
                def body(c, v):
                    start = pl.multiple_of(offset + c * width, NARROW)
                    return step(start, width, v)
                return body
            value = lax.fori_loop(0, wide, over(WIDE, 0), value)
            return lax.fori_loop(0, rest, over(NARROW, wide * WIDE), value)

        def score_step(start, width, m):
            at = pl.ds(start, width)
            s = mm_nt(q, ks[at, :])
            key = lax.broadcasted_iota(jnp.int32, (ROWS, width), 1) + start
            s = jnp.where(key <= rowpos[:, :1], s, F32(-1e30))
            scr[:, at] = s
            return jnp.maximum(m, fold(jnp.maximum, s))

        m = sweep(score_step, jnp.full((ROWS, DH), -1e30, F32))
        top = jnp.max(m, axis=1, keepdims=True)
        oacc[...] = jnp.zeros_like(oacc)

        def expo_step(start, width, tot):
            at = pl.ds(start, width)
            e = jnp.exp2((scr[:, at] - top) * F32(SCALE2))
            scr[:, at] = e
            oacc[...] += mm(e.astype(BF16), vs[at, :])
            return tot + fold(jnp.add, e)

        tot = sweep(expo_step, jnp.zeros((ROWS, DH), F32))
        total = jnp.sum(tot, axis=1, keepdims=True)
        inv = 1.0 / total
        att = (oacc[...] / total).astype(BF16)
        dsum = jnp.sum(gr.astype(F32) * att.astype(F32), axis=1, keepdims=True)
        qacc[...] = jnp.zeros_like(qacc)

        def back_step(start, width, carry):
            at = pl.ds(start, width)
            dp = mm_nt(gr, vs[at, :])
            p = scr[:, at] * inv
            ds = (p * (dp - dsum)).astype(BF16)
            qacc[...] += mm(ds, ks[at, :])
            dkt[:, at] += mm(q_t, ds)
            dvt[:, at] += mm(g_t, p.astype(BF16))
            return carry

        sweep(back_step, 0)
        dq = (qacc[...] * F32(SCALE)).astype(BF16)
        for k in range(GROUP):
            to = block_rows(sblk[base + k])
            stage_q[to, :DH] = att[k * BLK:(k + 1) * BLK, :]
            stage_q[to, DH:] = dq[k * BLK:(k + 1) * BLK, :]
        return carry

    lax.fori_loop(0, (per_part // GROUP) * busy, group_step, 0)

    for t in range(ks.shape[0] // DH):
        at = slice(t * DH, (t + 1) * DH)
        ks[at, :] = (dkt[:, at] * F32(SCALE)).T.astype(BF16)
        vs[at, :] = dvt[:, at].T.astype(BF16)

    sends = [pltpu.make_async_copy(stage_q, oq, out_sems.at[8])]
    sends[0].start()
    slots = (
        (o2a, 2, 0), (o2b, 2, half), (o3b, 3, half), (o1a, 1, 0), (o3a, 3, 0), (o1b, 1, half),
        (o0.at[:half * BLK], 0, 0), (o0.at[half * BLK:], 0, half),
    )
    for i, (out, part, first) in enumerate(slots):
        for j in range(half):
            at = block_rows(block_of(part, first + j))
            stage[i, j * BLK:(j + 1) * BLK, :DH] = ks[at, :]
            stage[i, j * BLK:(j + 1) * BLK, DH:] = vs[at, :]
        sends.append(pltpu.make_async_copy(stage.at[i], out, out_sems.at[i]))
        sends[-1].start()
    for copy in sends:
        copy.wait()


def attention(nz, nx, me, qg, kv, near, far):
    rows = qg.shape[0]
    seq = rows * nx
    sm = pl.BlockSpec(memory_space=pltpu.SMEM)
    anywhere = pl.BlockSpec(memory_space=pl.ANY)
    hbm = pl.BlockSpec(memory_space=pltpu.HBM)
    whole = pltpu.HBM((rows, 2 * DH), BF16)
    half = pltpu.HBM((rows // 2, 2 * DH), BF16)
    return pl.pallas_call(
        lambda *refs: attention_kernel(nz, nx, *refs),
        out_shape=(whole,) * 2 + (half,) * 6,
        in_specs=[sm] + [anywhere] * 8,
        out_specs=(hbm,) * 8,
        scratch_shapes=[
            pltpu.VMEM((seq, DH), BF16),
            pltpu.VMEM((seq, DH), BF16),
            pltpu.VMEM((rows, DH), BF16),
            pltpu.VMEM((rows, DH), BF16),
            pltpu.VMEM((ROWS, seq), F32),
            pltpu.VMEM((DH, seq), F32),
            pltpu.VMEM((DH, seq), F32),
            pltpu.VMEM((ROWS, DH), F32),
            pltpu.VMEM((ROWS, DH), F32),
            pltpu.VMEM((ROWS, DH), jnp.int32),
            pltpu.SMEM((rows // BLK,), jnp.int32),
            pltpu.SMEM((rows // BLK,), jnp.int32),
            pltpu.VMEM((rows, 2 * DH), BF16),
        ]
        + [pltpu.VMEM((rows // 2, 2 * DH), BF16)] * 6
        + [
            pltpu.VMEM((rows, 2 * DH), BF16),
            pltpu.VMEM((8, rows // 2, 2 * DH), BF16),
            pltpu.VMEM((rows, 2 * DH), BF16),
            pltpu.SemaphoreType.DMA((8,)),
            pltpu.SemaphoreType.DMA((9,)),
        ],
        compiler_params=pltpu.CompilerParams(vmem_limit_bytes=36 * 2**20),
        name="attention",
    )(me, kv, *near, *far, qg)


def by_head(pairs, slots):
    rows, width = pairs[0][0].shape
    heads = width // DH
    count = len(pairs)

    def kernel(*refs):
        ins, outs = refs[:2 * count], refs[2 * count:]
        for i, out in enumerate(outs):
            for slot in range(slots):
                head = (slot + 2 * heads - slots) % heads
                cols = slice(head * DH, (head + 1) * DH)
                out[slot, :, :DH] = ins[2 * i][:, cols]
                out[slot, :, DH:] = ins[2 * i + 1][:, cols]

    vm = pl.BlockSpec(memory_space=pltpu.VMEM)
    return pl.pallas_call(
        kernel,
        out_shape=(jax.ShapeDtypeStruct((slots, rows, 2 * DH), BF16),) * count,
        in_specs=[vm] * (2 * count),
        out_specs=(vm,) * count,
        name="by_head",
    )(*[array for pair in pairs for array in pair])


def from_heads(early, late, heads):
    slots, rows = late.shape[:2]
    first = slots - heads

    def kernel(early_ref, late_ref, a_ref, b_ref, c_ref, d_ref, got, a_own, b_own, c_own, d_own, sems):
        fetch = pltpu.make_async_copy(early_ref.at[first:], got, sems.at[0])
        fetch.start()
        sends = []

        def split(stack, skip, left, right, left_out, right_out):
            for head in range(heads):
                cols = slice(head * DH, (head + 1) * DH)
                left[:, cols] = stack[skip + head, :, :DH]
                right[:, cols] = stack[skip + head, :, DH:]
            for own, out in ((left, left_out), (right, right_out)):
                sends.append(pltpu.make_async_copy(own, out, sems.at[len(sends) + 1]))
                sends[-1].start()

        split(late_ref, first, c_own, d_own, c_ref, d_ref)
        fetch.wait()
        split(got, 0, a_own, b_own, a_ref, b_ref)
        for copy in sends:
            copy.wait()

    hbm = pl.BlockSpec(memory_space=pltpu.HBM)
    return pl.pallas_call(
        kernel,
        out_shape=(pltpu.HBM((rows, heads * DH), BF16),) * 4,
        in_specs=[pl.BlockSpec(memory_space=pl.ANY), pl.BlockSpec(memory_space=pltpu.VMEM)],
        out_specs=(hbm,) * 4,
        scratch_shapes=[pltpu.VMEM((heads, rows, 2 * DH), BF16)]
        + [pltpu.VMEM((rows, heads * DH), BF16)] * 4
        + [pltpu.SemaphoreType.DMA((5,))],
        name="from_heads",
    )(early, pltpu.with_memory_space_constraint(late, pltpu.VMEM))


def ring_orders(nz):
    first = list(range(0, nz, 2)) + list(range(nz - 1, 0, -2))
    turn = nz // 4
    return first, first[turn:] + first[:turn]


def make_shards(nz, nx):
    def to(step):
        return [(i, (i + step) % nx) for i in range(nx)]

    rings = ring_orders(nz)
    groups = [[z * len(rings) + core for z in ring] for core, ring in enumerate(rings)]

    def exchange(v):
        return lax.all_to_all(v, ("z", "kv"), 0, 0, axis_index_groups=groups, tiled=True)

    def shards(queries, keys, values, out_grad, block_order):
        rows, width = queries.shape[1:]
        heads = width // DH
        kv, qg = by_head(((keys[0], values[0]), (queries[0], out_grad[0])), nz)
        kv = exchange(kv).reshape(nz * rows, 2 * DH)
        cut = nz * rows // 2
        kva, kvb = kv[:cut], kv[cut:]
        right_a = lax.ppermute(kva, "x", to(1))
        left_b = lax.ppermute(kvb, "x", to(-1))
        right_b = lax.ppermute(kvb, "x", to(1))
        left_a = lax.ppermute(kva, "x", to(-1))
        far_a = lax.ppermute(right_a, "x", to(1))
        far_b = lax.ppermute(left_b, "x", to(-1))
        qg = exchange(qg).reshape(nz * rows, 2 * DH)
        ring = jnp.asarray(rings, jnp.int32)[lax.axis_index("kv")]
        idle = jnp.any(ring[:nz - heads] == lax.axis_index("z"))
        place = jnp.stack([lax.axis_index("x").astype(jnp.int32), 1 - idle.astype(jnp.int32)])
        me = jnp.concatenate([place, ring, block_order[0]])
        oq, o0, o1a, o1b, o2a, o2b, o3a, o3b = attention(
            nz, nx, me, qg, kv, (right_a, right_b, left_a, left_b), (far_a, far_b)
        )
        via_right = lax.ppermute(o2a, "x", to(1))
        via_left = lax.ppermute(o2b, "x", to(-1))
        r3b = lax.ppermute(o3b, "x", to(1))
        r1a = lax.ppermute(o1a, "x", to(-1))
        r3a = lax.ppermute(o3a + via_right, "x", to(1))
        r1b = lax.ppermute(o1b + via_left, "x", to(-1))
        early = exchange(oq.reshape(nz, rows, 2 * DH))
        total_a = (o0[:cut].astype(F32) + r1a.astype(F32) + r3a.astype(F32)).astype(BF16)
        total_b = (o0[cut:].astype(F32) + r1b.astype(F32) + r3b.astype(F32)).astype(BF16)
        total = jnp.concatenate([total_a, total_b], axis=0)
        late = exchange(total.reshape(nz, rows, 2 * DH))
        att, q_grad, k_grad, v_grad = from_heads(early, late, heads)
        return att[None], q_grad[None], k_grad[None], v_grad[None]

    return shards


def solution(mesh):
    sizes = dict(mesh.shape)
    nx = 4
    nz = sizes["pb"] // nx
    fine = Mesh(
        np.asarray(mesh.devices).reshape(nz, nx, sizes["kv"], sizes["ha"]), ("z", "x", "kv", "ha")
    )
    split = P("kv", ("z", "x"), "ha")
    return jax.shard_map(
        make_shards(nz, nx),
        mesh=fine,
        in_specs=(split, split, split, split, P("kv", None)),
        out_specs=(split,) * 4,
        check_vma=False,
    )
```

```python
import math

import jax
import jax.numpy as jnp
import numpy as np
from jax import lax
from jax.experimental import pallas as pl
from jax.experimental.pallas import tpu as pltpu
from jax.sharding import Mesh
from jax.sharding import PartitionSpec as P

DH = 128
BLK = 64
SCALE = 1.0 / math.sqrt(DH)
SCALE2 = SCALE * math.log2(math.e)
GROUP = 8
ROWS = GROUP * BLK
WIDE = 2048
NARROW = 512
F32 = jnp.float32
BF16 = jnp.bfloat16


def mm(a, b):
    return jnp.dot(a, b, preferred_element_type=F32)


def mm_nt(a, b):
    return lax.dot_general(a, b, (((1,), (1,)), ((), ())), preferred_element_type=F32)


def attention_kernel(
    nz, nx, me, in0, in1, in2, in3, in4, in5, in6, in7,
    oq, o0, o1a, o1b, o2a, o2b, o3a, o3b,
    ks, vs, qs, gs, scr, dkt, dvt, qacc, oacc, rowpos, sblk, spos,
    kv0, kv1a, kv1b, kv3a, kv3b, kv2a, kv2b, qg, stage, stage_q, in_sems, out_sems,
):
    arrays = (in0, in1, in2, in3, in4, in5, in6, in7)
    landed = (kv0, kv1a, kv1b, kv3a, kv3b, kv2a, kv2b, qg)
    fetch = [
        pltpu.make_async_copy(src, dst, in_sems.at[i])
        for i, (src, dst) in enumerate(zip(arrays, landed, strict=True))
    ]
    for copy in fetch:
        copy.start()
    x = me[0]
    busy = me[1]
    order = me.at[2 + nz:]
    per_part = 2 * nz
    half = per_part // 2

    def block_of(part, j):
        src = lax.rem(x - part + nx, nx)
        return order[(me[2 + j // 2] * nx + src) * 2 + j % 2]

    def block_rows(p):
        return pl.ds(pl.multiple_of(p * BLK, BLK), BLK)

    def part_ref(full, a, b, j):
        if full is not None:
            return full, j * BLK
        return (a, j * BLK) if j < half else (b, (j - half) * BLK)

    pieces = ((None, None), (kv1a, kv1b), (kv2a, kv2b), (kv3a, kv3b))
    arrivals = {0: (0,), 1: (1, 2), 3: (3, 4), 2: (5, 6)}
    for part in (0, 1, 3, 2):
        for i in arrivals[part]:
            fetch[i].wait()
        for j in range(per_part):
            ref, start = part_ref(kv0 if part == 0 else None, *pieces[part], j)
            at = block_rows(block_of(part, j))
            ks[at, :] = ref[start:start + BLK, :DH]
            vs[at, :] = ref[start:start + BLK, DH:]

    fetch[7].wait()
    own = [block_of(0, j) for j in range(per_part)]
    for j in range(per_part):
        rank = jnp.int32(0)
        for i in range(per_part):
            if i != j:
                rank = rank + (own[i] < own[j]).astype(jnp.int32)
        sblk[rank] = jnp.int32(j)
        spos[rank] = own[j]
        at = block_rows(rank)
        qs[at, :] = qg[j * BLK:(j + 1) * BLK, :DH]
        gs[at, :] = qg[j * BLK:(j + 1) * BLK, DH:]

    dkt[...] = jnp.zeros_like(dkt)
    dvt[...] = jnp.zeros_like(dvt)

    def fold(op, s):
        r = s[:, :DH]
        for i in range(1, s.shape[1] // DH):
            r = op(r, s[:, i * DH:(i + 1) * DH])
        return r

    def group_step(g, carry):
        base = g * GROUP
        tiles = ((spos[base + GROUP - 1] + 1) * BLK + NARROW - 1) // NARROW
        wide = tiles // (WIDE // NARROW)
        rest = tiles % (WIDE // NARROW)
        for k in range(GROUP):
            within = lax.broadcasted_iota(jnp.int32, (BLK, DH), 0)
            rowpos[k * BLK:(k + 1) * BLK, :] = within + spos[base + k] * BLK
        at = pl.ds(pl.multiple_of(base * BLK, ROWS), ROWS)
        q = qs[at, :]
        gr = gs[at, :]
        q_t = q.T
        g_t = gr.T

        def sweep(step, value):
            def over(width, offset):
                def body(c, v):
                    start = pl.multiple_of(offset + c * width, NARROW)
                    return step(start, width, v)
                return body
            value = lax.fori_loop(0, wide, over(WIDE, 0), value)
            return lax.fori_loop(0, rest, over(NARROW, wide * WIDE), value)

        def score_step(start, width, m):
            at = pl.ds(start, width)
            s = mm_nt(q, ks[at, :])
            key = lax.broadcasted_iota(jnp.int32, (ROWS, width), 1) + start
            s = jnp.where(key <= rowpos[:, :1], s, F32(-1e30))
            scr[:, at] = s
            return jnp.maximum(m, fold(jnp.maximum, s))

        m = sweep(score_step, jnp.full((ROWS, DH), -1e30, F32))
        top = jnp.max(m, axis=1, keepdims=True)
        oacc[...] = jnp.zeros_like(oacc)

        def expo_step(start, width, tot):
            at = pl.ds(start, width)
            e = jnp.exp2((scr[:, at] - top) * F32(SCALE2))
            scr[:, at] = e
            oacc[...] += mm(e.astype(BF16), vs[at, :])
            return tot + fold(jnp.add, e)

        tot = sweep(expo_step, jnp.zeros((ROWS, DH), F32))
        total = jnp.sum(tot, axis=1, keepdims=True)
        inv = 1.0 / total
        att = (oacc[...] / total).astype(BF16)
        dsum = jnp.sum(gr.astype(F32) * att.astype(F32), axis=1, keepdims=True)
        qacc[...] = jnp.zeros_like(qacc)

        def back_step(start, width, carry):
            at = pl.ds(start, width)
            dp = mm_nt(gr, vs[at, :])
            p = scr[:, at] * inv
            ds = (p * (dp - dsum)).astype(BF16)
            qacc[...] += mm(ds, ks[at, :])
            dkt[:, at] += mm(q_t, ds)
            dvt[:, at] += mm(g_t, p.astype(BF16))
            return carry

        sweep(back_step, 0)
        dq = (qacc[...] * F32(SCALE)).astype(BF16)
        for k in range(GROUP):
            to = block_rows(sblk[base + k])
            stage_q[to, :DH] = att[k * BLK:(k + 1) * BLK, :]
            stage_q[to, DH:] = dq[k * BLK:(k + 1) * BLK, :]
        return carry

    lax.fori_loop(0, (per_part // GROUP) * busy, group_step, 0)

    for t in range(ks.shape[0] // DH):
        at = slice(t * DH, (t + 1) * DH)
        ks[at, :] = (dkt[:, at] * F32(SCALE)).T.astype(BF16)
        vs[at, :] = dvt[:, at].T.astype(BF16)

    sends = [pltpu.make_async_copy(stage_q, oq, out_sems.at[8])]
    sends[0].start()
    slots = (
        (o2a, 2, 0), (o2b, 2, half), (o3b, 3, half), (o1a, 1, 0), (o3a, 3, 0), (o1b, 1, half),
        (o0.at[:half * BLK], 0, 0), (o0.at[half * BLK:], 0, half),
    )
    for i, (out, part, first) in enumerate(slots):
        for j in range(half):
            at = block_rows(block_of(part, first + j))
            stage[i, j * BLK:(j + 1) * BLK, :DH] = ks[at, :]
            stage[i, j * BLK:(j + 1) * BLK, DH:] = vs[at, :]
        sends.append(pltpu.make_async_copy(stage.at[i], out, out_sems.at[i]))
        sends[-1].start()
    for copy in sends:
        copy.wait()


def attention(nz, nx, me, qg, kv, near, far):
    rows = qg.shape[0]
    seq = rows * nx
    sm = pl.BlockSpec(memory_space=pltpu.SMEM)
    anywhere = pl.BlockSpec(memory_space=pl.ANY)
    hbm = pl.BlockSpec(memory_space=pltpu.HBM)
    whole = pltpu.HBM((rows, 2 * DH), BF16)
    half = pltpu.HBM((rows // 2, 2 * DH), BF16)
    return pl.pallas_call(
        lambda *refs: attention_kernel(nz, nx, *refs),
        out_shape=(whole,) * 2 + (half,) * 6,
        in_specs=[sm] + [anywhere] * 8,
        out_specs=(hbm,) * 8,
        scratch_shapes=[
            pltpu.VMEM((seq, DH), BF16),
            pltpu.VMEM((seq, DH), BF16),
            pltpu.VMEM((rows, DH), BF16),
            pltpu.VMEM((rows, DH), BF16),
            pltpu.VMEM((ROWS, seq), F32),
            pltpu.VMEM((DH, seq), F32),
            pltpu.VMEM((DH, seq), F32),
            pltpu.VMEM((ROWS, DH), F32),
            pltpu.VMEM((ROWS, DH), F32),
            pltpu.VMEM((ROWS, DH), jnp.int32),
            pltpu.SMEM((rows // BLK,), jnp.int32),
            pltpu.SMEM((rows // BLK,), jnp.int32),
            pltpu.VMEM((rows, 2 * DH), BF16),
        ]
        + [pltpu.VMEM((rows // 2, 2 * DH), BF16)] * 6
        + [
            pltpu.VMEM((rows, 2 * DH), BF16),
            pltpu.VMEM((8, rows // 2, 2 * DH), BF16),
            pltpu.VMEM((rows, 2 * DH), BF16),
            pltpu.SemaphoreType.DMA((8,)),
            pltpu.SemaphoreType.DMA((9,)),
        ],
        compiler_params=pltpu.CompilerParams(vmem_limit_bytes=36 * 2**20),
        name="attention",
    )(me, kv, *near, *far, qg)


def by_head(pairs, slots):
    rows, width = pairs[0][0].shape
    heads = width // DH
    count = len(pairs)

    def kernel(*refs):
        ins, outs = refs[:2 * count], refs[2 * count:3 * count]
        got, packed, sems = refs[3 * count:]
        fetch = [
            pltpu.make_async_copy(src, got.at[i], sems.at[i]) for i, src in enumerate(ins)
        ]
        for copy in fetch:
            copy.start()
        sends = []
        for i, out in enumerate(outs):
            fetch[2 * i].wait()
            fetch[2 * i + 1].wait()
            for slot in range(slots):
                head = (slot + 2 * heads - slots) % heads
                cols = slice(head * DH, (head + 1) * DH)
                packed[i, slot, :, :DH] = got[2 * i, :, cols]
                packed[i, slot, :, DH:] = got[2 * i + 1, :, cols]
            sends.append(pltpu.make_async_copy(packed.at[i], out, sems.at[2 * count + i]))
            sends[-1].start()
        for copy in sends:
            copy.wait()

    anywhere = pl.BlockSpec(memory_space=pl.ANY)
    hbm = pl.BlockSpec(memory_space=pltpu.HBM)
    return pl.pallas_call(
        kernel,
        out_shape=(pltpu.HBM((slots, rows, 2 * DH), BF16),) * count,
        in_specs=[anywhere] * (2 * count),
        out_specs=(hbm,) * count,
        scratch_shapes=[
            pltpu.VMEM((2 * count, rows, width), BF16),
            pltpu.VMEM((count, slots, rows, 2 * DH), BF16),
            pltpu.SemaphoreType.DMA((3 * count,)),
        ],
        name="by_head",
    )(*[array for pair in pairs for array in pair])


def from_heads(early, late, heads):
    slots, rows = late.shape[:2]
    first = slots - heads

    def kernel(early_ref, late_ref, a_ref, b_ref, c_ref, d_ref, got, sems):
        fetch = pltpu.make_async_copy(early_ref.at[first:], got, sems.at[0])
        fetch.start()
        sends = []

        def split(stack, skip, left_out, right_out):
            for head in range(heads):
                cols = slice(head * DH, (head + 1) * DH)
                for out, at in ((left_out, slice(0, DH)), (right_out, slice(DH, 2 * DH))):
                    sends.append(
                        pltpu.make_async_copy(
                            stack.at[skip + head, :, at], out.at[:, cols], sems.at[len(sends) + 1]
                        )
                    )
                    sends[-1].start()

        split(late_ref, first, c_ref, d_ref)
        fetch.wait()
        split(got, 0, a_ref, b_ref)
        for copy in sends:
            copy.wait()

    hbm = pl.BlockSpec(memory_space=pltpu.HBM)
    return pl.pallas_call(
        kernel,
        out_shape=(pltpu.HBM((rows, heads * DH), BF16),) * 4,
        in_specs=[pl.BlockSpec(memory_space=pl.ANY), pl.BlockSpec(memory_space=pltpu.VMEM)],
        out_specs=(hbm,) * 4,
        scratch_shapes=[
            pltpu.VMEM((heads, rows, 2 * DH), BF16),
            pltpu.SemaphoreType.DMA((4 * heads + 1,)),
        ],
        name="from_heads",
    )(early, pltpu.with_memory_space_constraint(late, pltpu.VMEM))


def ring_orders(nz):
    first = list(range(0, nz, 2)) + list(range(nz - 1, 0, -2))
    turn = nz // 4
    return first, first[turn:] + first[:turn]


def make_shards(nz, nx):
    def to(step):
        return [(i, (i + step) % nx) for i in range(nx)]

    rings = ring_orders(nz)
    groups = [[z * len(rings) + core for z in ring] for core, ring in enumerate(rings)]

    def exchange(v):
        return lax.all_to_all(v, ("z", "kv"), 0, 0, axis_index_groups=groups, tiled=True)

    def shards(queries, keys, values, out_grad, block_order):
        rows, width = queries.shape[1:]
        heads = width // DH
        (kv,) = by_head(((keys[0], values[0]),), nz)
        (qg,) = by_head(((queries[0], out_grad[0]),), nz)
        kv = exchange(kv).reshape(nz * rows, 2 * DH)
        cut = nz * rows // 2
        kva, kvb = kv[:cut], kv[cut:]
        right_a = lax.ppermute(kva, "x", to(1))
        left_b = lax.ppermute(kvb, "x", to(-1))
        right_b = lax.ppermute(kvb, "x", to(1))
        left_a = lax.ppermute(kva, "x", to(-1))
        far_a = lax.ppermute(right_a, "x", to(1))
        far_b = lax.ppermute(left_b, "x", to(-1))
        qg = exchange(qg).reshape(nz * rows, 2 * DH)
        ring = jnp.asarray(rings, jnp.int32)[lax.axis_index("kv")]
        idle = jnp.any(ring[:nz - heads] == lax.axis_index("z"))
        place = jnp.stack([lax.axis_index("x").astype(jnp.int32), 1 - idle.astype(jnp.int32)])
        me = jnp.concatenate([place, ring, block_order[0]])
        oq, o0, o1a, o1b, o2a, o2b, o3a, o3b = attention(
            nz, nx, me, qg, kv, (right_a, right_b, left_a, left_b), (far_a, far_b)
        )
        via_right = lax.ppermute(o2a, "x", to(1))
        via_left = lax.ppermute(o2b, "x", to(-1))
        r3b = lax.ppermute(o3b, "x", to(1))
        r1a = lax.ppermute(o1a, "x", to(-1))
        r3a = lax.ppermute(o3a + via_right, "x", to(1))
        r1b = lax.ppermute(o1b + via_left, "x", to(-1))
        early = exchange(oq.reshape(nz, rows, 2 * DH))
        total_a = (o0[:cut].astype(F32) + r1a.astype(F32) + r3a.astype(F32)).astype(BF16)
        total_b = (o0[cut:].astype(F32) + r1b.astype(F32) + r3b.astype(F32)).astype(BF16)
        total = jnp.concatenate([total_a, total_b], axis=0)
        late = exchange(total.reshape(nz, rows, 2 * DH))
        att, q_grad, k_grad, v_grad = from_heads(early, late, heads)
        return att[None], q_grad[None], k_grad[None], v_grad[None]

    return shards


def solution(mesh):
    sizes = dict(mesh.shape)
    nx = 4
    nz = sizes["pb"] // nx
    fine = Mesh(
        np.asarray(mesh.devices).reshape(nz, nx, sizes["kv"], sizes["ha"]), ("z", "x", "kv", "ha")
    )
    split = P("kv", ("z", "x"), "ha")
    return jax.shard_map(
        make_shards(nz, nx),
        mesh=fine,
        in_specs=(split, split, split, split, P("kv", None)),
        out_specs=(split,) * 4,
        check_vma=False,
    )
```

```python
import math

import jax
import jax.numpy as jnp
import numpy as np
from jax import lax
from jax.experimental import pallas as pl
from jax.experimental.pallas import tpu as pltpu
from jax.sharding import Mesh
from jax.sharding import PartitionSpec as P

DH = 128
BLK = 64
SCALE = 1.0 / math.sqrt(DH)
SCALE2 = SCALE * math.log2(math.e)
GROUP = 4
ROWS = GROUP * BLK
WIDE = 2048
F32 = jnp.float32
BF16 = jnp.bfloat16


def mm(a, b):
    return jnp.dot(a, b, preferred_element_type=F32)


def mm_nt(a, b):
    return lax.dot_general(a, b, (((1,), (1,)), ((), ())), preferred_element_type=F32)


def attention_kernel(
    nz, nx, me, in0, in1, in2, in3, in4, in5, in6, in7,
    oq, o0, o1a, o1b, o2a, o2b, o3a, o3b,
    ks, vs, qs, gs, scr, dkt, dvt, qacc, oacc, acc_m, acc_l, q_t, g_t, rowpos, sblk, spos,
    kv0, kv1a, kv1b, kv3a, kv3b, kv2a, kv2b, qg, stage, stage_q, in_sems, out_sems,
):
    arrays = (in0, in1, in2, in3, in4, in5, in6, in7)
    landed = (kv0, kv1a, kv1b, kv3a, kv3b, kv2a, kv2b, qg)
    fetch = [
        pltpu.make_async_copy(src, dst, in_sems.at[i])
        for i, (src, dst) in enumerate(zip(arrays, landed, strict=True))
    ]
    for copy in fetch:
        copy.start()
    x = me[0]
    busy = me[1]
    order = me.at[2 + nz:]
    per_part = 2 * nz
    half = per_part // 2

    def block_of(part, j):
        src = lax.rem(x - part + nx, nx)
        return order[(me[2 + j // 2] * nx + src) * 2 + j % 2]

    def block_rows(p):
        return pl.ds(pl.multiple_of(p * BLK, BLK), BLK)

    def part_ref(full, a, b, j):
        if full is not None:
            return full, j * BLK
        return (a, j * BLK) if j < half else (b, (j - half) * BLK)

    pieces = ((None, None), (kv1a, kv1b), (kv2a, kv2b), (kv3a, kv3b))
    arrivals = {0: (0,), 1: (1, 2), 3: (3, 4), 2: (5, 6)}
    for part in (0, 1, 3, 2):
        for i in arrivals[part]:
            fetch[i].wait()
        for j in range(per_part):
            ref, start = part_ref(kv0 if part == 0 else None, *pieces[part], j)
            at = block_rows(block_of(part, j))
            ks[at, :] = ref[start:start + BLK, :DH]
            vs[at, :] = ref[start:start + BLK, DH:]

    fetch[7].wait()
    own = [block_of(0, j) for j in range(per_part)]
    for j in range(per_part):
        rank = jnp.int32(0)
        for i in range(per_part):
            if i != j:
                rank = rank + (own[i] < own[j]).astype(jnp.int32)
        sblk[rank] = jnp.int32(j)
        spos[rank] = own[j]
        at = block_rows(rank)
        qs[at, :] = qg[j * BLK:(j + 1) * BLK, :DH]
        gs[at, :] = qg[j * BLK:(j + 1) * BLK, DH:]

    rows = per_part * BLK
    for k in range(per_part):
        within = lax.broadcasted_iota(jnp.int32, (BLK, DH), 0)
        rowpos[k * BLK:(k + 1) * BLK, :] = within + spos[k] * BLK
    q_t[...] = qs[...].T
    g_t[...] = gs[...].T
    acc_m[...] = jnp.full_like(acc_m, -1e30)
    acc_l[...] = jnp.zeros_like(acc_l)
    oacc[...] = jnp.zeros_like(oacc)
    qacc[...] = jnp.zeros_like(qacc)

    def fold(op, s):
        r = s[:, :DH]
        for i in range(1, s.shape[1] // DH):
            r = op(r, s[:, i * DH:(i + 1) * DH])
        return r

    def sweep(step, empty=None):
        def chunk(c, carry):
            start = pl.multiple_of(c * WIDE, WIDE)
            late = jnp.int32(0)
            for k in range(per_part):
                late = late + (spos[k] * BLK + (BLK - 1) >= start).astype(jnp.int32)
            steps = (late + GROUP - 1) // GROUP
            for v in range(1, per_part // GROUP + 1):
                @pl.when(steps == v)
                def _(v=v):
                    step(pl.ds(start, WIDE), start, slice(rows - v * ROWS, rows))
            if empty is not None:
                @pl.when(steps == 0)
                def _():
                    empty(pl.ds(start, WIDE))
            return carry

        lax.fori_loop(0, (ks.shape[0] // WIDE) * busy, chunk, 0)

    def score_step(at, start, low):
        s = mm_nt(qs[low, :], ks[at, :])
        key = lax.broadcasted_iota(jnp.int32, s.shape, 1) + start
        s = jnp.where(key <= rowpos[low, :1], s, F32(-1e30))
        scr[low, at] = s
        acc_m[low, :] = jnp.maximum(acc_m[low, :], fold(jnp.maximum, s))

    sweep(score_step)
    acc_m[...] = jnp.broadcast_to(jnp.max(acc_m[...], axis=1, keepdims=True), acc_m.shape)

    def expo_step(at, start, low):
        e = jnp.exp2((scr[low, at] - acc_m[low, :1]) * F32(SCALE2))
        scr[low, at] = e
        oacc[low, :] += mm(e.astype(BF16), vs[at, :])
        acc_l[low, :] += fold(jnp.add, e)

    sweep(expo_step)
    total = jnp.sum(acc_l[...], axis=1, keepdims=True)
    att = (oacc[...] / total).astype(BF16)
    dsum = jnp.sum(gs[...].astype(F32) * att.astype(F32), axis=1, keepdims=True)
    acc_m[...] = jnp.broadcast_to(1.0 / total, acc_m.shape)
    acc_l[...] = jnp.broadcast_to(dsum, acc_l.shape)

    def back_step(at, start, low):
        dp = mm_nt(gs[low, :], vs[at, :])
        p = scr[low, at] * acc_m[low, :1]
        ds = (p * (dp - acc_l[low, :1])).astype(BF16)
        qacc[low, :] += mm(ds, ks[at, :])
        dkt[:, at] = mm(q_t[:, low], ds)
        dvt[:, at] = mm(g_t[:, low], p.astype(BF16))

    def no_rows(at):
        dkt[:, at] = jnp.zeros((DH, WIDE), F32)
        dvt[:, at] = jnp.zeros((DH, WIDE), F32)

    sweep(back_step, no_rows)
    dq = (qacc[...] * F32(SCALE)).astype(BF16)
    for k in range(per_part):
        to = block_rows(sblk[k])
        stage_q[to, :DH] = att[k * BLK:(k + 1) * BLK, :]
        stage_q[to, DH:] = dq[k * BLK:(k + 1) * BLK, :]

    for t in range(ks.shape[0] // DH):
        at = slice(t * DH, (t + 1) * DH)
        ks[at, :] = (dkt[:, at] * F32(SCALE)).T.astype(BF16)
        vs[at, :] = dvt[:, at].T.astype(BF16)

    sends = [pltpu.make_async_copy(stage_q, oq, out_sems.at[8])]
    sends[0].start()
    slots = (
        (o2a, 2, 0), (o2b, 2, half), (o3b, 3, half), (o1a, 1, 0), (o3a, 3, 0), (o1b, 1, half),
        (o0.at[:half * BLK], 0, 0), (o0.at[half * BLK:], 0, half),
    )
    for i, (out, part, first) in enumerate(slots):
        for j in range(half):
            at = block_rows(block_of(part, first + j))
            stage[i, j * BLK:(j + 1) * BLK, :DH] = ks[at, :]
            stage[i, j * BLK:(j + 1) * BLK, DH:] = vs[at, :]
        sends.append(pltpu.make_async_copy(stage.at[i], out, out_sems.at[i]))
        sends[-1].start()
    for copy in sends:
        copy.wait()


def attention(nz, nx, me, qg, kv, near, far):
    rows = qg.shape[0]
    seq = rows * nx
    sm = pl.BlockSpec(memory_space=pltpu.SMEM)
    anywhere = pl.BlockSpec(memory_space=pl.ANY)
    hbm = pl.BlockSpec(memory_space=pltpu.HBM)
    whole = pltpu.HBM((rows, 2 * DH), BF16)
    half = pltpu.HBM((rows // 2, 2 * DH), BF16)
    return pl.pallas_call(
        lambda *refs: attention_kernel(nz, nx, *refs),
        out_shape=(whole,) * 2 + (half,) * 6,
        in_specs=[sm] + [anywhere] * 8,
        out_specs=(hbm,) * 8,
        scratch_shapes=[
            pltpu.VMEM((seq, DH), BF16),
            pltpu.VMEM((seq, DH), BF16),
            pltpu.VMEM((rows, DH), BF16),
            pltpu.VMEM((rows, DH), BF16),
            pltpu.VMEM((rows, seq), F32),
            pltpu.VMEM((DH, seq), F32),
            pltpu.VMEM((DH, seq), F32),
            pltpu.VMEM((rows, DH), F32),
            pltpu.VMEM((rows, DH), F32),
            pltpu.VMEM((rows, DH), F32),
            pltpu.VMEM((rows, DH), F32),
            pltpu.VMEM((DH, rows), BF16),
            pltpu.VMEM((DH, rows), BF16),
            pltpu.VMEM((rows, DH), jnp.int32),
            pltpu.SMEM((rows // BLK,), jnp.int32),
            pltpu.SMEM((rows // BLK,), jnp.int32),
            pltpu.VMEM((rows, 2 * DH), BF16),
        ]
        + [pltpu.VMEM((rows // 2, 2 * DH), BF16)] * 6
        + [
            pltpu.VMEM((rows, 2 * DH), BF16),
            pltpu.VMEM((8, rows // 2, 2 * DH), BF16),
            pltpu.VMEM((rows, 2 * DH), BF16),
            pltpu.SemaphoreType.DMA((8,)),
            pltpu.SemaphoreType.DMA((9,)),
        ],
        compiler_params=pltpu.CompilerParams(vmem_limit_bytes=48 * 2**20),
        name="attention",
    )(me, kv, *near, *far, qg)


def by_head(pairs, slots):
    rows, width = pairs[0][0].shape
    heads = width // DH
    count = len(pairs)

    def kernel(*refs):
        ins, outs = refs[:2 * count], refs[2 * count:3 * count]
        got, packed, sems = refs[3 * count:]
        fetch = [
            pltpu.make_async_copy(src, got.at[i], sems.at[i]) for i, src in enumerate(ins)
        ]
        for copy in fetch:
            copy.start()
        sends = []
        for i, out in enumerate(outs):
            fetch[2 * i].wait()
            fetch[2 * i + 1].wait()
            for slot in range(slots):
                head = (slot + 2 * heads - slots) % heads
                cols = slice(head * DH, (head + 1) * DH)
                packed[i, slot, :, :DH] = got[2 * i, :, cols]
                packed[i, slot, :, DH:] = got[2 * i + 1, :, cols]
            sends.append(pltpu.make_async_copy(packed.at[i], out, sems.at[2 * count + i]))
            sends[-1].start()
        for copy in sends:
            copy.wait()

    anywhere = pl.BlockSpec(memory_space=pl.ANY)
    hbm = pl.BlockSpec(memory_space=pltpu.HBM)
    return pl.pallas_call(
        kernel,
        out_shape=(pltpu.HBM((slots, rows, 2 * DH), BF16),) * count,
        in_specs=[anywhere] * (2 * count),
        out_specs=(hbm,) * count,
        scratch_shapes=[
            pltpu.VMEM((2 * count, rows, width), BF16),
            pltpu.VMEM((count, slots, rows, 2 * DH), BF16),
            pltpu.SemaphoreType.DMA((3 * count,)),
        ],
        name="by_head",
    )(*[array for pair in pairs for array in pair])


def from_heads(early, late, heads):
    slots, rows = late.shape[:2]
    first = slots - heads

    def kernel(early_ref, late_ref, a_ref, b_ref, c_ref, d_ref, got, sems):
        fetch = pltpu.make_async_copy(early_ref.at[first:], got, sems.at[0])
        fetch.start()
        sends = []

        def split(stack, skip, left_out, right_out):
            for head in range(heads):
                cols = slice(head * DH, (head + 1) * DH)
                for out, at in ((left_out, slice(0, DH)), (right_out, slice(DH, 2 * DH))):
                    sends.append(
                        pltpu.make_async_copy(
                            stack.at[skip + head, :, at], out.at[:, cols], sems.at[len(sends) + 1]
                        )
                    )
                    sends[-1].start()

        split(late_ref, first, c_ref, d_ref)
        fetch.wait()
        split(got, 0, a_ref, b_ref)
        for copy in sends:
            copy.wait()

    hbm = pl.BlockSpec(memory_space=pltpu.HBM)
    return pl.pallas_call(
        kernel,
        out_shape=(pltpu.HBM((rows, heads * DH), BF16),) * 4,
        in_specs=[pl.BlockSpec(memory_space=pl.ANY), pl.BlockSpec(memory_space=pltpu.VMEM)],
        out_specs=(hbm,) * 4,
        scratch_shapes=[
            pltpu.VMEM((heads, rows, 2 * DH), BF16),
            pltpu.SemaphoreType.DMA((4 * heads + 1,)),
        ],
        name="from_heads",
    )(early, pltpu.with_memory_space_constraint(late, pltpu.VMEM))


def ring_orders(nz):
    first = list(range(0, nz, 2)) + list(range(nz - 1, 0, -2))
    turn = nz // 4
    return first, first[turn:] + first[:turn]


def make_shards(nz, nx):
    def to(step):
        return [(i, (i + step) % nx) for i in range(nx)]

    rings = ring_orders(nz)
    groups = [[z * len(rings) + core for z in ring] for core, ring in enumerate(rings)]

    def exchange(v):
        return lax.all_to_all(v, ("z", "kv"), 0, 0, axis_index_groups=groups, tiled=True)

    def shards(queries, keys, values, out_grad, block_order):
        rows, width = queries.shape[1:]
        heads = width // DH
        (kv,) = by_head(((keys[0], values[0]),), nz)
        (qg,) = by_head(((queries[0], out_grad[0]),), nz)
        kv = exchange(kv).reshape(nz * rows, 2 * DH)
        cut = nz * rows // 2
        kva, kvb = kv[:cut], kv[cut:]
        right_a = lax.ppermute(kva, "x", to(1))
        left_b = lax.ppermute(kvb, "x", to(-1))
        right_b = lax.ppermute(kvb, "x", to(1))
        left_a = lax.ppermute(kva, "x", to(-1))
        far_a = lax.ppermute(right_a, "x", to(1))
        far_b = lax.ppermute(left_b, "x", to(-1))
        qg = exchange(qg).reshape(nz * rows, 2 * DH)
        ring = jnp.asarray(rings, jnp.int32)[lax.axis_index("kv")]
        idle = jnp.any(ring[:nz - heads] == lax.axis_index("z"))
        place = jnp.stack([lax.axis_index("x").astype(jnp.int32), 1 - idle.astype(jnp.int32)])
        me = jnp.concatenate([place, ring, block_order[0]])
        oq, o0, o1a, o1b, o2a, o2b, o3a, o3b = attention(
            nz, nx, me, qg, kv, (right_a, right_b, left_a, left_b), (far_a, far_b)
        )
        via_right = lax.ppermute(o2a, "x", to(1))
        via_left = lax.ppermute(o2b, "x", to(-1))
        r3b = lax.ppermute(o3b, "x", to(1))
        r1a = lax.ppermute(o1a, "x", to(-1))
        r3a = lax.ppermute(o3a + via_right, "x", to(1))
        r1b = lax.ppermute(o1b + via_left, "x", to(-1))
        early = exchange(oq.reshape(nz, rows, 2 * DH))
        total_a = (o0[:cut].astype(F32) + r1a.astype(F32) + r3a.astype(F32)).astype(BF16)
        total_b = (o0[cut:].astype(F32) + r1b.astype(F32) + r3b.astype(F32)).astype(BF16)
        total = jnp.concatenate([total_a, total_b], axis=0)
        late = exchange(total.reshape(nz, rows, 2 * DH))
        att, q_grad, k_grad, v_grad = from_heads(early, late, heads)
        return att[None], q_grad[None], k_grad[None], v_grad[None]

    return shards


def solution(mesh):
    sizes = dict(mesh.shape)
    nx = 4
    nz = sizes["pb"] // nx
    fine = Mesh(
        np.asarray(mesh.devices).reshape(nz, nx, sizes["kv"], sizes["ha"]), ("z", "x", "kv", "ha")
    )
    split = P("kv", ("z", "x"), "ha")
    return jax.shard_map(
        make_shards(nz, nx),
        mesh=fine,
        in_specs=(split, split, split, split, P("kv", None)),
        out_specs=(split,) * 4,
        check_vma=False,
    )
```
